256 devices in a mesh: ctx: 32 (over z_lo, x, y), tp: 8 (over z_hi, core).
Axes of the slice: x: 4, y: 4, z: 8 (z_hi: 4, z_lo: 2; z = z_hi * 2 + z_lo), core: 2. Of those that a mesh axis runs over, the one named last changes fastest.
Arguments:
- out_grad: bfloat16 [8192, 4096], P('ctx', 'tp'), may hold values from -6 to 6
- gate_act: bfloat16 [8192, 4096], P('ctx', 'tp'), may hold values from -6 to 6
- key_act: bfloat16 [8192, 4096], P('ctx', 'tp'), may hold values from -6 to 6
- value_act: bfloat16 [8192, 4096], P('ctx', 'tp'), may hold values from -6 to 6
- filter_taps: float32 [8192, 4096], P('ctx', 'tp'), may hold values from -6 to 6
- out_weight: bfloat16 [4096, 4096], P('tp'), may hold values from -0.09375 to 0.09375
Outputs:
- grad_gate: bfloat16 [8192, 4096], P('ctx', 'tp')
- grad_key: bfloat16 [8192, 4096], P('ctx', 'tp')
- grad_value: bfloat16 [8192, 4096], P('ctx', 'tp')
- grad_taps: float32 [8192, 4096], P('ctx', 'tp')
The draws below stay inside these ranges and needn't reach their ends.
All inputs are finite; a program needn't handle non-finite values.
Results may differ from the reference program's by a relative error of at most 0.012.
Values may be sent and summed in bfloat16 or wider, within the bound.
No kernel may reach another device: no remote copies, remote signals or barrier semaphores. Data moves between devices by JAX's collectives and lax.ppermute only.
A program may use at most 128 MiB of HBM per device.

```python
import math
import jax
import jax.numpy as jnp

D = 4096
TOKENS = 8192


def block_scale(own_key, extent, pieces, least, high):
    def one(dim, blocks):
        draws = jax.random.uniform(jax.random.fold_in(jax.random.fold_in(own_key, 6), dim), (blocks,), jnp.float32, least / len(pieces), high / len(pieces))
        return jnp.repeat(jnp.exp(draws), extent[dim] // blocks).reshape((-1,) + (1,) * (len(extent) - dim - 1))

    loudness = one(*pieces[0])
    for cut in pieces[1:]:
        loudness = loudness * one(*cut)
    return loudness


def centred(own_key, extent, scale, bound, split=(), held_as=jnp.bfloat16):
    level = block_scale(own_key, extent, split, -0.22, 0.18) if split else 1.0
    array = jax.random.normal(own_key, extent, jnp.float32) * scale * level
    return jnp.minimum(jnp.maximum(array, -bound), bound).astype(held_as)


def setup_inputs(seed: int = 0) -> dict:
    key_of = jax.random.split(jax.random.key(seed), 7)
    return {
        "out_grad": centred(key_of[0], (TOKENS, D), 1.0, 6.0, ((0, 32), (1, 8))),
        "gate_act": centred(key_of[1], (TOKENS, D), 1.0, 6.0, ((0, 32), (1, 8))),
        "key_act": centred(key_of[2], (TOKENS, D), 1.0, 6.0, ((0, 32), (1, 8))),
        "value_act": centred(key_of[3], (TOKENS, D), 1.0, 6.0, ((0, 32), (1, 8))),
        "filter_taps": centred(key_of[4], (TOKENS, D), 1.0, 6.0, ((0, 32), (1, 8)), jnp.float32),
        "out_weight": centred(key_of[5], (D, D), D ** -0.5, 0.09375, ((0, 8),)),
    }


def reference(out_grad, gate_act, key_act, value_act, filter_taps, out_weight):
    grad_mix = jnp.dot(out_grad, out_weight.T, preferred_element_type=jnp.float32).astype(jnp.bfloat16)
    mixed_full = grad_mix.astype(jnp.float32)
    gate_full = gate_act.astype(jnp.float32)
    key_full = key_act.astype(jnp.float32)
    value_full = value_act.astype(jnp.float32)
    inner_prod = key_full * value_full
    tap_scale = 1.0 / math.sqrt(TOKENS)
    impulse = filter_taps * tap_scale
    grad_conv = mixed_full * gate_full
    span_length = 2 * TOKENS
    spec_inner = jnp.fft.rfft(inner_prod, n=span_length, axis=0)
    spec_impulse = jnp.fft.rfft(impulse, n=span_length, axis=0)
    spec_grad = jnp.fft.rfft(grad_conv, n=span_length, axis=0)
    conv_out = jnp.fft.irfft(spec_impulse * spec_inner, n=span_length, axis=0)[:TOKENS]
    grad_inner = jnp.fft.irfft(jnp.conj(spec_impulse) * spec_grad, n=span_length, axis=0)[:TOKENS]
    grad_impulse = jnp.fft.irfft(jnp.conj(spec_inner) * spec_grad, n=span_length, axis=0)[:TOKENS]
    grad_gate = (mixed_full * conv_out).astype(jnp.bfloat16)
    grad_key = (grad_inner * value_full).astype(jnp.bfloat16)
    grad_value = (grad_inner * key_full).astype(jnp.bfloat16)
    grad_taps = (grad_impulse * tap_scale).astype(jnp.float32)
    return (grad_gate, grad_key, grad_value, grad_taps)
```

```python
import math

import jax
import jax.numpy as jnp
import ml_dtypes
import numpy as np
from jax import lax
from jax.experimental import pallas as pl
from jax.experimental.pallas import tpu as pltpu
from jax.sharding import PartitionSpec as P

BF = jnp.bfloat16
F32 = jnp.float32
PARTS = 32
ROWS = 256
CHANS = 16
TOKENS = PARTS * ROWS
CHUNKS = 4
STEP = PARTS // CHUNKS
HALF = STEP * CHANS


def tables():
    k1 = np.arange(PARTS)
    r = np.arange(ROWS)
    first = 2.0 * np.pi * (((4 * k1[:, None] + 1) * k1[None, :]) % (4 * PARTS)) / (4 * PARTS)
    twist = 2.0 * np.pi * (((4 * k1[:, None] + 1) * r[None, :]) % (4 * TOKENS)) / (4 * TOKENS)
    second = 2.0 * np.pi * ((r[:, None] * r[None, :]) % ROWS) / ROWS
    eye = np.eye(CHANS)
    rows = []
    for i in range(CHUNKS):
        part = first[i * STEP : (i + 1) * STEP]
        rows += [np.kron(np.cos(part), eye), np.kron(-np.sin(part), eye)]
    spread = np.concatenate(rows, 0)
    cos, sin = np.cos(second), np.sin(second)
    ahead = np.block([[cos, -sin], [sin, cos]])
    back = np.block([[cos, sin], [-sin, cos]])
    wide = lambda a: np.ascontiguousarray(
        np.broadcast_to(a[:, None, :], (PARTS, 8, ROWS))
    ).astype(np.float32)
    half = lambda a: np.ascontiguousarray(a).astype(ml_dtypes.bfloat16)
    return (
        half(spread),
        half(spread.T),
        half(ahead),
        half(back),
        wide(np.cos(twist)),
        wide(np.sin(twist)),
    )


def dot(a, b):
    return lax.dot_general(a, b, (((1,), (0,)), ((), ())), preferred_element_type=F32)


def dot_t(a, b):
    return lax.dot_general(a, b, (((1,), (1,)), ((), ())), preferred_element_type=F32)


def turn(re, im, cos, sin):
    re = re.reshape(STEP, 2, 8, ROWS)
    im = im.reshape(STEP, 2, 8, ROWS)
    cos, sin = cos[:, None], sin[:, None]
    out_re = (re * cos - im * sin).astype(BF).reshape(HALF, ROWS)
    out_im = (im * cos + re * sin).astype(BF).reshape(HALF, ROWS)
    return out_re, out_im


def forward(signal, i, spread, ahead, cos, sin):
    a = dot(spread[2 * HALF * i : 2 * HALF * (i + 1), :], signal)
    part = slice(i * STEP, (i + 1) * STEP)
    re, im = turn(a[:HALF], a[HALF:], cos[part], -sin[part])
    return dot(jnp.concatenate([re, im], 1), ahead[...])


def inverse(re, im, i, back, cos, sin, held, slot):
    z = dot(jnp.concatenate([re.astype(BF), im.astype(BF)], 1), back[...])
    part = slice(i * STEP, (i + 1) * STEP)
    re, im = turn(z[:, :ROWS], z[:, ROWS:], cos[part], sin[part])
    held[slot, 2 * HALF * i : 2 * HALF * i + HALF, :] = re
    held[slot, 2 * HALF * i + HALF : 2 * HALF * (i + 1), :] = im


SCALE = 1.0 / (math.sqrt(TOKENS) * TOKENS)


def collect(gather, held, slot):
    return (dot(gather[...], held[slot]) * SCALE).astype(BF).reshape(PARTS, CHANS, ROWS)


def prepare_kernel(key, value, taps, out):
    inner = key[...].astype(F32) * value[...].astype(F32)
    out[:, 0] = inner.T.astype(BF).reshape(PARTS, CHANS, ROWS)
    out[:, 1] = taps[...].T.astype(BF).reshape(PARTS, CHANS, ROWS)


def early_kernel(got, spread, gather, ahead, back, cos, sin, spec, conv, held):
    inner = got[:, 0].reshape(PARTS * CHANS, ROWS)
    taps = got[:, 1].reshape(PARTS * CHANS, ROWS)
    for i in range(CHUNKS):
        x = forward(inner, i, spread, ahead, cos, sin)
        h = forward(taps, i, spread, ahead, cos, sin)
        spec[0, HALF * i : HALF * (i + 1), :] = x
        spec[1, HALF * i : HALF * (i + 1), :] = h
        xr, xi, hr, hi = x[:, :ROWS], x[:, ROWS:], h[:, :ROWS], h[:, ROWS:]
        inverse(hr * xr - hi * xi, hr * xi + hi * xr, i, back, cos, sin, held, 0)
    conv[...] = collect(gather, held, 0)


def late_kernel(got, spec, conv, spread, gather, ahead, back, cos, sin, out, held):
    out[:, 0] = conv[...]
    grad = got[...].reshape(PARTS * CHANS, ROWS)
    for i in range(CHUNKS):
        g = forward(grad, i, spread, ahead, cos, sin)
        rows = slice(HALF * i, HALF * (i + 1))
        gr, gi = g[:, :ROWS], g[:, ROWS:]
        xr, xi = spec[0, rows, :ROWS], spec[0, rows, ROWS:]
        hr, hi = spec[1, rows, :ROWS], spec[1, rows, ROWS:]
        inverse(hr * gr + hi * gi, hr * gi - hi * gr, i, back, cos, sin, held, 0)
        inverse(xr * gr + xi * gi, xr * gi - xi * gr, i, back, cos, sin, held, 1)
    out[:, 1] = collect(gather, held, 0)
    out[:, 2] = collect(gather, held, 1)


def first_mix_kernel(ids, weight, *refs):
    blocks, out = refs[:-1], refs[-1]
    total = None
    for n, block in enumerate(blocks):
        width = block.shape[1]
        columns = pl.ds(pl.multiple_of(ids[n] * width, width), width)
        term = dot_t(block[...], weight[:, columns])
        total = term if total is None else total + term
    out[...] = total


def last_mix_kernel(ids, total, far, far_pair, weight, weight_pair, gate, mix, out):
    del ids
    sums = total[...] + dot_t(far[...], weight[...]) + dot_t(far_pair[...], weight_pair[...])
    mixed = sums.astype(BF)
    mix[...] = mixed
    grad = mixed.astype(F32) * gate[...].astype(F32)
    out[...] = grad.T.astype(BF).reshape(PARTS, CHANS, ROWS)


def finish_kernel(got, mix, key, value, grad_gate, grad_key, grad_value, grad_taps):
    def result(slot):
        return got[:, slot].reshape(PARTS * CHANS, ROWS).astype(F32).T

    grad_gate[...] = (mix[...].astype(F32) * result(0)).astype(BF)
    inner = result(1)
    grad_key[...] = (inner * value[...].astype(F32)).astype(BF)
    grad_value[...] = (inner * key[...].astype(F32)).astype(BF)
    grad_taps[...] = result(2)


PARAMS = pltpu.CompilerParams(vmem_limit_bytes=48 * 1024 * 1024)


def call(kernel, outs, *args, scratch=(), flops=0):
    nbytes = sum(a.size * a.dtype.itemsize for a in (*args, *jax.tree.leaves(outs)))
    return pl.pallas_call(
        kernel,
        out_shape=outs,
        scratch_shapes=scratch,
        compiler_params=PARAMS,
        cost_estimate=pl.CostEstimate(flops=flops, bytes_accessed=nbytes, transcendentals=0),
    )(*args)


def shape(dims, dtype=BF):
    return jax.ShapeDtypeStruct(dims, dtype)


def shards(out_grad, gate_act, key_act, value_act, filter_taps, out_weight):
    count = lax.axis_size("tp")
    me = lax.axis_index("tp")

    def ring(block, steps):
        return lax.ppermute(block, "tp", [(i, (i + steps) % count) for i in range(count)])

    def swap(block):
        return lax.ppermute(block, "tp", [(i, i ^ 1) for i in range(count)])

    def exchange(block):
        return lax.all_to_all(block, "ctx", split_axis=0, concat_axis=0, tiled=True)

    spread, gather, ahead, back, cos, sin = (jnp.asarray(t) for t in tables())
    block = (PARTS, CHANS, ROWS)
    rows, chans = gate_act.shape

    right = ring(out_grad, 2)
    left = ring(out_grad, -2)
    far = ring(out_grad, 4)
    pair = swap(out_grad)

    sent = call(prepare_kernel, shape((PARTS, 2, CHANS, ROWS)), key_act, value_act, filter_taps)
    got = exchange(sent)
    held = lambda n: [pltpu.VMEM((n, 2 * PARTS * CHANS, ROWS), BF)]
    spec, conv = call(
        early_kernel,
        (shape((2, PARTS * CHANS, 2 * ROWS), F32), shape(block)),
        got, spread, gather, ahead, back, cos, sin,
        scratch=held(1), flops=1_600_000_000,
    )

    offsets = jnp.array([0, 0, -2, -2, 2, 2, 4, 4], jnp.int32)
    flips = jnp.array([0, 1, 0, 1, 0, 1, 0, 1], jnp.int32)
    ids = ((me ^ flips) + offsets) % count
    smem = pl.BlockSpec(memory_space=pltpu.SMEM)
    blocks = (out_grad, pair, right, swap(right), left, swap(left))
    total = pl.pallas_call(
        first_mix_kernel,
        out_shape=shape((rows, chans), F32),
        in_specs=[smem] + [pl.BlockSpec(memory_space=pltpu.VMEM)] * (1 + len(blocks)),
        compiler_params=PARAMS,
        cost_estimate=pl.CostEstimate(flops=800_000_000, bytes_accessed=6_000_000, transcendentals=0),
    )(ids, out_weight, *blocks)

    whole = lambda dims: pl.BlockSpec(dims, lambda i, ids: (0,) * len(dims))
    mix, sent = pl.pallas_call(
        last_mix_kernel,
        out_shape=(shape((rows, chans)), shape(block)),
        grid_spec=pltpu.PrefetchScalarGridSpec(
            num_scalar_prefetch=1,
            grid=(1,),
            in_specs=[
                whole((rows, chans)),
                whole((rows, chans)),
                whole((rows, chans)),
                pl.BlockSpec((chans, chans), lambda i, ids: (0, ids[6])),
                pl.BlockSpec((chans, chans), lambda i, ids: (0, ids[7])),
                whole((rows, chans)),
            ],
            out_specs=[whole((rows, chans)), whole(block)],
        ),
        compiler_params=PARAMS,
        cost_estimate=pl.CostEstimate(flops=270_000_000, bytes_accessed=3_000_000, transcendentals=0),
    )(ids, total, far, swap(far), out_weight, out_weight, gate_act)

    got = exchange(sent)
    sent = call(
        late_kernel,
        shape((PARTS, 3, CHANS, ROWS)),
        got, spec, conv, spread, gather, ahead, back, cos, sin,
        scratch=held(2), flops=1_600_000_000,
    )
    got = exchange(sent)
    return call(
        finish_kernel,
        (shape((rows, chans)), shape((rows, chans)), shape((rows, chans)), shape((rows, chans), F32)),
        got, mix, key_act, value_act,
    )


def solution(mesh):
    in_specs = (
        P("ctx", "tp"),
        P("ctx", "tp"),
        P("ctx", "tp"),
        P("ctx", "tp"),
        P("ctx", "tp"),
        P("tp", None),
    )
    out_specs = (P("ctx", "tp"), P("ctx", "tp"), P("ctx", "tp"), P("ctx", "tp"))
    return jax.shard_map(shards, mesh=mesh, in_specs=in_specs, out_specs=out_specs, check_vma=False)
```

```python
import math

import jax
import jax.numpy as jnp
import ml_dtypes
import numpy as np
from jax import lax
from jax.experimental import pallas as pl
from jax.experimental.pallas import tpu as pltpu
from jax.sharding import PartitionSpec as P

BF = jnp.bfloat16
F32 = jnp.float32
PARTS = 32
ROWS = 256
CHANS = 16
TOKENS = PARTS * ROWS
HALF = CHANS // 2
WIDE = PARTS * HALF
SCALE = 1.0 / (math.sqrt(TOKENS) * TOKENS)


def tables():
    k1 = np.arange(PARTS)
    r = np.arange(ROWS)
    first = 2.0 * np.pi * (((4 * k1[:, None] + 1) * k1[None, :]) % (4 * PARTS)) / (4 * PARTS)
    twist = 2.0 * np.pi * (((4 * k1[:, None] + 1) * r[None, :]) % (4 * TOKENS)) / (4 * TOKENS)
    second = 2.0 * np.pi * ((r[:, None] * r[None, :]) % ROWS) / ROWS
    eye = np.eye(HALF)
    spread_re, spread_im = np.kron(np.cos(first), eye), np.kron(-np.sin(first), eye)
    gather = np.concatenate([spread_re.T, spread_im.T], 1)
    cos, sin = np.cos(second), np.sin(second)
    ahead = np.block([[cos, -sin], [sin, cos]])
    packed = np.concatenate([ahead, gather, np.concatenate([spread_re, spread_im], 1)], 0)
    wide = lambda a: np.broadcast_to(a[:, None, :], (PARTS, HALF, ROWS)).reshape(WIDE, ROWS)
    twists = np.stack([wide(np.cos(twist)), wide(np.sin(twist))])
    return packed.astype(ml_dtypes.bfloat16), twists.astype(np.float32)


def dot(a, b):
    return lax.dot_general(a, b, (((1,), (0,)), ((), ())), preferred_element_type=F32)


def dot_t(a, b):
    return lax.dot_general(a, b, (((1,), (1,)), ((), ())), preferred_element_type=F32)


def forward(signal, table, twists):
    re = dot(table[2 * ROWS + WIDE :, :WIDE], signal)
    im = dot(table[2 * ROWS + WIDE :, WIDE:], signal)
    cos, sin = twists[0], twists[1]
    turned = jnp.concatenate([(re * cos + im * sin).astype(BF), (im * cos - re * sin).astype(BF)], 1)
    out = dot(turned, table[: 2 * ROWS, :])
    return out[:, :ROWS], out[:, ROWS:]


def inverse(re, minus_im, table, twists):
    out = dot(jnp.concatenate([re.astype(BF), minus_im.astype(BF)], 1), table[: 2 * ROWS, :])
    re, minus_im = out[:, :ROWS], out[:, ROWS:]
    cos, sin = twists[0], twists[1]
    turned_re = (re * cos + minus_im * sin).astype(BF)
    turned_im = (re * sin - minus_im * cos).astype(BF)
    back = dot(table[2 * ROWS : 2 * ROWS + WIDE, :], jnp.concatenate([turned_re, turned_im], 0))
    return (back * SCALE).reshape(PARTS, HALF, ROWS)


def half_rows(block, half):
    rows = block.astype(F32).reshape(PARTS, 2, HALF, ROWS)[:, half]
    return rows.reshape(WIDE, ROWS).astype(BF)


def whole(halves):
    return jnp.stack(halves, 1).reshape(PARTS, CHANS, ROWS).astype(BF)


KEPT = 5


def early_kernel(source, table, twists, kept, got, sem):
    load = pltpu.make_async_copy(source, got, sem)
    load.start()
    load.wait()
    for half in range(2):
        xr, xi = forward(half_rows(got[:, 0], half), table, twists)
        hr, hi = forward(half_rows(got[:, 1], half), table, twists)
        conv = inverse(hr * xr - hi * xi, -(hr * xi + hi * xr), table, twists)
        for n, part in enumerate((xr, xi, hr, hi, conv.reshape(WIDE, ROWS))):
            kept[half * KEPT + n] = part


def late_kernel(got, kept, table, twists, out):
    results = []
    for half in range(2):
        gr, gi = forward(half_rows(got[...], half), table, twists)
        xr, xi, hr, hi, conv = (kept[half * KEPT + n] for n in range(KEPT))
        results.append((
            conv.reshape(PARTS, HALF, ROWS),
            inverse(hr * gr + hi * gi, hi * gr - hr * gi, table, twists),
            inverse(xr * gr + xi * gi, xi * gr - xr * gi, table, twists),
        ))
    for n in range(3):
        out[:, n] = whole([results[0][n], results[1][n]])


def columns(step, flip, width):
    holder = lax.axis_index("tp") ^ flip
    count = lax.axis_size("tp")
    way = 1 - 2 * lax.rem(holder, 2)
    owner = lax.rem(holder - 2 * step * way + count, count)
    return pl.ds(pl.multiple_of(owner * width, width), width)


def prepare_kernel(
    key, value, taps, own, weight, table, twists, pair,
    out, total, table_out, twists_out, k, v, t, o, w, sent, sems,
):
    width = own.shape[1]
    loads = [(key, k), (value, v), (taps, t), (own, o)]
    loads += [(weight.at[:, columns(0, flip, width)], w.at[flip]) for flip in range(2)]
    loads += [(table, table_out), (twists, twists_out)]
    loads = [pltpu.make_async_copy(*ends, sems.at[n]) for n, ends in enumerate(loads)]
    for load in loads:
        load.start()
    for load in loads[:2]:
        load.wait()
    inner = k[...].astype(F32) * v[...].astype(F32)
    sent[:, 0] = inner.T.astype(BF).reshape(PARTS, CHANS, ROWS)
    loads[2].wait()
    sent[:, 1] = t[...].T.astype(BF).reshape(PARTS, CHANS, ROWS)
    store = pltpu.make_async_copy(sent, out, sems.at[8])
    store.start()
    for load in loads[3:6]:
        load.wait()
    total[...] = dot_t(o[...], w[0]) + dot_t(pair[...], w[1])
    for load in loads[6:]:
        load.wait()
    store.wait()


def first_mix_kernel(weight, before, ahead, ahead_pair, behind, behind_pair, total, later, w, sems):
    width = ahead.shape[1]
    loads = []
    for n, (step, flip) in enumerate(((1, 0), (1, 1), (-1, 0), (-1, 1), (2, 0), (2, 1))):
        target = w.at[n] if n < 4 else later.at[n - 4]
        loads.append(
            pltpu.make_async_copy(weight.at[:, columns(step, flip, width)], target, sems.at[n])
        )
        loads[n].start()
    sums = before[...]
    for n, block in enumerate((ahead, ahead_pair, behind, behind_pair)):
        loads[n].wait()
        sums = sums + dot_t(block[...], w[n])
    total[...] = sums
    loads[4].wait()
    loads[5].wait()


def last_mix_kernel(weight, total, far, far_pair, gate, mix, out, mixed, sem):
    sums = total[...] + dot_t(far[...], weight[0]) + dot_t(far_pair[...], weight[1])
    mixed[...] = sums.astype(BF)
    store = pltpu.make_async_copy(mixed, mix, sem)
    store.start()
    grad = sums.astype(BF).astype(F32) * gate[...].astype(F32)
    out[...] = grad.T.astype(BF).reshape(PARTS, CHANS, ROWS)
    store.wait()


def finish_kernel(got, mix, key, value, *refs):
    outs, results, sems = refs[:4], refs[4:8], refs[8]

    def result(slot):
        return got[:, slot].reshape(PARTS * CHANS, ROWS).astype(F32).T

    def store(n):
        copy = pltpu.make_async_copy(results[n], outs[n], sems.at[n])
        copy.start()
        return copy

    results[3][...] = result(2)
    copies = [store(3)]
    inner = result(1)
    results[1][...] = (inner * value[...].astype(F32)).astype(BF)
    copies.append(store(1))
    results[2][...] = (inner * key[...].astype(F32)).astype(BF)
    copies.append(store(2))
    results[0][...] = (mix[...].astype(F32) * result(0)).astype(BF)
    copies.append(store(0))
    for copy in copies:
        copy.wait()


PARAMS = pltpu.CompilerParams(vmem_limit_bytes=40 * 1024 * 1024)


def call(kernel, outs, *args, spaces, scratch=(), flops=0):
    leaves = jax.tree.leaves(outs)
    nbytes = sum(a.size * a.dtype.itemsize for a in (*args, *leaves))
    spaces = [pltpu.HBM if letter == "h" else pltpu.VMEM for letter in spaces]
    specs = [pl.BlockSpec(memory_space=space) for space in spaces]
    args = [pltpu.with_memory_space_constraint(a, space) for a, space in zip(args, spaces)]
    placed = [space(a.shape, a.dtype) for a, space in zip(leaves, spaces[len(args) :])]
    results = pl.pallas_call(
        kernel,
        out_shape=placed,
        in_specs=specs[: len(args)],
        out_specs=specs[len(args) :],
        scratch_shapes=scratch,
        compiler_params=PARAMS,
        cost_estimate=pl.CostEstimate(flops=flops, bytes_accessed=nbytes, transcendentals=0),
    )(*args)
    return results if isinstance(outs, tuple) else results[0]


def shape(dims, dtype=BF):
    return jax.ShapeDtypeStruct(dims, dtype)


def shards(out_grad, gate_act, key_act, value_act, filter_taps, out_weight):
    count = lax.axis_size("tp")
    rows, chans = gate_act.shape

    def ring(block, way):
        hops = [(i, (i + way * (2 - 4 * (i % 2))) % count) for i in range(count)]
        return lax.ppermute(block, "tp", hops)

    def swap(block):
        return lax.ppermute(block, "tp", [(i, i ^ 1) for i in range(count)])

    def exchange(block):
        return lax.all_to_all(block, "ctx", split_axis=0, concat_axis=0, tiled=True)

    table, twists = (jnp.asarray(t) for t in tables())
    together = lax.optimization_barrier
    block = shape((PARTS, CHANS, ROWS))
    partial = shape((rows, chans), F32)
    held = pltpu.VMEM((rows, chans), BF)
    weights = lambda n: (n, chans, chans)
    sems = pltpu.SemaphoreType.DMA((14,))

    ahead = ring(out_grad, 1)
    pair = swap(out_grad)
    again, pair = together((out_grad, pair))
    behind = ring(again, -1)
    sent, total, table, twists = call(
        prepare_kernel,
        (shape((PARTS, 2, CHANS, ROWS)), partial, shape(table.shape), shape(twists.shape, F32)),
        key_act, value_act, filter_taps, out_grad, out_weight, table, twists, pair,
        spaces="hhhhhhhv" + "hvvv",
        scratch=[
            held, held, pltpu.VMEM((rows, chans), F32), held, pltpu.VMEM(weights(2), BF),
            pltpu.VMEM((PARTS, 2, CHANS, ROWS), BF), sems,
        ],
        flops=270_000_000,
    )
    got = exchange(sent)
    ahead, total = together((ahead, total))
    far = ring(ahead, 1)
    ahead, behind = together((ahead, behind))
    total, later = call(
        first_mix_kernel, (partial, shape(weights(2))),
        out_weight, total, ahead, swap(ahead), behind, swap(behind),
        spaces="hvvvvv" + "vv",
        scratch=[pltpu.VMEM(weights(4), BF), sems], flops=7_000_000_000,
    )
    kept = call(
        early_kernel, shape((2 * KEPT, WIDE, ROWS), F32), got, table, twists,
        spaces="hvv" + "v",
        scratch=[pltpu.VMEM((PARTS, 2, CHANS, ROWS), BF), pltpu.SemaphoreType.DMA],
        flops=1_200_000_000,
    )
    far, total, kept = together((far, total, kept))
    mix, sent = call(
        last_mix_kernel, (shape((rows, chans)), block),
        later, total, far, swap(far), gate_act,
        spaces="vvvvv" + "hv",
        scratch=[held, pltpu.SemaphoreType.DMA], flops=300_000_000_000,
    )
    got = exchange(sent)
    sent = call(
        late_kernel, shape((PARTS, 3, CHANS, ROWS)), got, kept, table, twists,
        spaces="vvvv" + "v", flops=1_200_000_000,
    )
    got = exchange(sent)
    return tuple(call(
        finish_kernel,
        (shape((rows, chans)), shape((rows, chans)), shape((rows, chans)), shape((rows, chans), F32)),
        got, mix, key_act, value_act,
        spaces="vvvv" + "hhhh",
        scratch=[held, held, held, pltpu.VMEM((rows, chans), F32), pltpu.SemaphoreType.DMA((4,))],
    ))


def solution(mesh):
    in_specs = (
        P("ctx", "tp"),
        P("ctx", "tp"),
        P("ctx", "tp"),
        P("ctx", "tp"),
        P("ctx", "tp"),
        P("tp", None),
    )
    out_specs = (P("ctx", "tp"), P("ctx", "tp"), P("ctx", "tp"), P("ctx", "tp"))
    return jax.shard_map(shards, mesh=mesh, in_specs=in_specs, out_specs=out_specs, check_vma=False)
```

```python
import math

import jax
import jax.numpy as jnp
import ml_dtypes
import numpy as np
from jax import lax
from jax.experimental import pallas as pl
from jax.experimental.pallas import tpu as pltpu
from jax.sharding import PartitionSpec as P

BF = jnp.bfloat16
F32 = jnp.float32
PARTS = 32
ROWS = 256
CHANS = 16
TOKENS = PARTS * ROWS
HALF = CHANS // 2
WIDE = PARTS * HALF
SCALE = 1.0 / (math.sqrt(TOKENS) * TOKENS)


def tables():
    k1 = np.arange(PARTS)
    r = np.arange(ROWS)
    first = 2.0 * np.pi * (((4 * k1[:, None] + 1) * k1[None, :]) % (4 * PARTS)) / (4 * PARTS)
    twist = 2.0 * np.pi * (((4 * k1[:, None] + 1) * r[None, :]) % (4 * TOKENS)) / (4 * TOKENS)
    second = 2.0 * np.pi * ((r[:, None] * r[None, :]) % ROWS) / ROWS
    eye = np.eye(HALF)
    spread_re, spread_im = np.kron(np.cos(first), eye), np.kron(-np.sin(first), eye)
    gather = np.concatenate([spread_re.T, spread_im.T], 1)
    cos, sin = np.cos(second), np.sin(second)
    ahead = np.block([[cos, -sin], [sin, cos]])
    packed = np.concatenate([ahead, gather, np.concatenate([spread_re, spread_im], 1)], 0)
    wide = lambda a: np.broadcast_to(a[:, None, :], (PARTS, HALF, ROWS)).reshape(WIDE, ROWS)
    twists = np.stack([wide(np.cos(twist)), wide(np.sin(twist))])
    return packed.astype(ml_dtypes.bfloat16), twists.astype(np.float32)


def dot(a, b):
    return lax.dot_general(a, b, (((1,), (0,)), ((), ())), preferred_element_type=F32)


def dot_t(a, b):
    return lax.dot_general(a, b, (((1,), (1,)), ((), ())), preferred_element_type=F32)


def spectra(signals, table, twists):
    cos, sin = twists[0], twists[1]
    turned = []
    for signal in signals:
        re = dot(table[2 * ROWS + WIDE :, :WIDE], signal)
        im = dot(table[2 * ROWS + WIDE :, WIDE:], signal)
        turned.append(
            jnp.concatenate([(re * cos + im * sin).astype(BF), (im * cos - re * sin).astype(BF)], 1)
        )
    return dot(jnp.concatenate(turned, 0), table[: 2 * ROWS, :])


def inverses(pairs, table, twists):
    rows = [jnp.concatenate([re.astype(BF), minus_im.astype(BF)], 1) for re, minus_im in pairs]
    out = dot(jnp.concatenate(rows, 0), table[: 2 * ROWS, :])
    cos, sin = twists[0], twists[1]
    results = []
    for n in range(len(pairs)):
        re = out[n * WIDE : (n + 1) * WIDE, :ROWS]
        minus_im = out[n * WIDE : (n + 1) * WIDE, ROWS:]
        turned_re = (re * cos + minus_im * sin).astype(BF)
        turned_im = (re * sin - minus_im * cos).astype(BF)
        back = dot(table[2 * ROWS : 2 * ROWS + WIDE, :], jnp.concatenate([turned_re, turned_im], 0))
        results.append((back * SCALE).reshape(PARTS, HALF, ROWS))
    return results


def halves(block):
    rows = block.astype(F32).reshape(PARTS, 2, HALF, ROWS)
    return [rows[:, half].reshape(WIDE, ROWS).astype(BF) for half in range(2)]


def whole(parts):
    return jnp.stack(parts, 1).reshape(PARTS, CHANS, ROWS).astype(BF)


KEPT = 5


def early_kernel(got, table, twists, kept):
    out = spectra(halves(got[:, 0]) + halves(got[:, 1]), table, twists)
    pairs = []
    for half in range(2):
        x, h = out[half * WIDE : (half + 1) * WIDE], out[(half + 2) * WIDE : (half + 3) * WIDE]
        xr, xi, hr, hi = x[:, :ROWS], x[:, ROWS:], h[:, :ROWS], h[:, ROWS:]
        for n, part in enumerate((xr, xi, hr, hi)):
            kept[half * KEPT + n] = part
        pairs.append((hr * xr - hi * xi, -(hr * xi + hi * xr)))
    for half, conv in enumerate(inverses(pairs, table, twists)):
        kept[half * KEPT + 4] = conv.reshape(WIDE, ROWS)


def late_kernel(got, kept, table, twists, out):
    out[:, 0] = whole([kept[half * KEPT + 4].reshape(PARTS, HALF, ROWS) for half in range(2)])
    grad = spectra(halves(got[...]), table, twists)
    pairs = []
    for half in range(2):
        g = grad[half * WIDE : (half + 1) * WIDE]
        gr, gi = g[:, :ROWS], g[:, ROWS:]
        xr, xi, hr, hi = (kept[half * KEPT + n] for n in range(4))
        pairs.append((hr * gr + hi * gi, hi * gr - hr * gi))
        pairs.append((xr * gr + xi * gi, xi * gr - xr * gi))
    results = inverses(pairs, table, twists)
    out[:, 1] = whole([results[0], results[2]])
    out[:, 2] = whole([results[1], results[3]])


def columns(step, flip, width):
    holder = lax.axis_index("tp") ^ flip
    count = lax.axis_size("tp")
    way = 1 - 2 * lax.rem(holder, 2)
    owner = lax.rem(holder - 2 * step * way + count, count)
    return pl.ds(pl.multiple_of(owner * width, width), width)


def prepare_kernel(
    key, value, taps, own, weight, table, twists, pair,
    out, total, table_out, twists_out, k, v, t, o, w, sent, sems,
):
    width = own.shape[1]
    loads = [(key, k), (value, v), (taps, t), (own, o)]
    loads += [(weight.at[:, columns(0, flip, width)], w.at[flip]) for flip in range(2)]
    loads += [(table, table_out), (twists, twists_out)]
    loads = [pltpu.make_async_copy(*ends, sems.at[n]) for n, ends in enumerate(loads)]
    for load in loads:
        load.start()
    for load in loads[:2]:
        load.wait()
    inner = k[...].astype(F32) * v[...].astype(F32)
    sent[:, 0] = inner.T.astype(BF).reshape(PARTS, CHANS, ROWS)
    loads[2].wait()
    sent[:, 1] = t[...].T.astype(BF).reshape(PARTS, CHANS, ROWS)
    store = pltpu.make_async_copy(sent, out, sems.at[8])
    store.start()
    for load in loads[3:6]:
        load.wait()
    total[...] = dot_t(o[...], w[0]) + dot_t(pair[...], w[1])
    for load in loads[6:]:
        load.wait()
    store.wait()


def first_mix_kernel(weight, before, ahead, ahead_pair, behind, behind_pair, total, later, w, sems):
    width = ahead.shape[1]
    loads = []
    for n, (step, flip) in enumerate(((1, 0), (1, 1), (-1, 0), (-1, 1), (2, 0), (2, 1))):
        target = w.at[n] if n < 4 else later.at[n - 4]
        loads.append(
            pltpu.make_async_copy(weight.at[:, columns(step, flip, width)], target, sems.at[n])
        )
        loads[n].start()
    sums = before[...]
    for n, block in enumerate((ahead, ahead_pair, behind, behind_pair)):
        loads[n].wait()
        sums = sums + dot_t(block[...], w[n])
    total[...] = sums
    loads[4].wait()
    loads[5].wait()


def last_mix_kernel(weight, total, far, far_pair, gate, mix, out, mixed, sem):
    sums = total[...] + dot_t(far[...], weight[0]) + dot_t(far_pair[...], weight[1])
    mixed[...] = sums.astype(BF)
    store = pltpu.make_async_copy(mixed, mix, sem)
    store.start()
    grad = sums.astype(BF).astype(F32) * gate[...].astype(F32)
    out[...] = grad.T.astype(BF).reshape(PARTS, CHANS, ROWS)
    store.wait()


def finish_kernel(got, mix, key, value, *refs):
    outs, results, sems = refs[:4], refs[4:8], refs[8]

    def result(slot):
        return got[:, slot].reshape(PARTS * CHANS, ROWS).astype(F32).T

    def store(n):
        copy = pltpu.make_async_copy(results[n], outs[n], sems.at[n])
        copy.start()
        return copy

    results[3][...] = result(2)
    copies = [store(3)]
    inner = result(1)
    results[1][...] = (inner * value[...].astype(F32)).astype(BF)
    copies.append(store(1))
    results[2][...] = (inner * key[...].astype(F32)).astype(BF)
    copies.append(store(2))
    results[0][...] = (mix[...].astype(F32) * result(0)).astype(BF)
    copies.append(store(0))
    for copy in copies:
        copy.wait()


PARAMS = pltpu.CompilerParams(vmem_limit_bytes=40 * 1024 * 1024)


def call(kernel, outs, *args, spaces, scratch=(), flops=0):
    leaves = jax.tree.leaves(outs)
    nbytes = sum(a.size * a.dtype.itemsize for a in (*args, *leaves))
    spaces = [pltpu.HBM if letter == "h" else pltpu.VMEM for letter in spaces]
    specs = [pl.BlockSpec(memory_space=space) for space in spaces]
    args = [pltpu.with_memory_space_constraint(a, space) for a, space in zip(args, spaces)]
    placed = [space(a.shape, a.dtype) for a, space in zip(leaves, spaces[len(args) :])]
    results = pl.pallas_call(
        kernel,
        out_shape=placed,
        in_specs=specs[: len(args)],
        out_specs=specs[len(args) :],
        scratch_shapes=scratch,
        compiler_params=PARAMS,
        cost_estimate=pl.CostEstimate(flops=flops, bytes_accessed=nbytes, transcendentals=0),
    )(*args)
    return results if isinstance(outs, tuple) else results[0]


def shape(dims, dtype=BF):
    return jax.ShapeDtypeStruct(dims, dtype)


def shards(out_grad, gate_act, key_act, value_act, filter_taps, out_weight):
    count = lax.axis_size("tp")
    rows, chans = gate_act.shape

    def ring(block, way):
        hops = [(i, (i + way * (2 - 4 * (i % 2))) % count) for i in range(count)]
        return lax.ppermute(block, "tp", hops)

    def swap(block):
        return lax.ppermute(block, "tp", [(i, i ^ 1) for i in range(count)])

    def exchange(block):
        return lax.all_to_all(block, "ctx", split_axis=0, concat_axis=0, tiled=True)

    table, twists = (jnp.asarray(t) for t in tables())
    together = lax.optimization_barrier
    block = shape((PARTS, CHANS, ROWS))
    partial = shape((rows, chans), F32)
    held = pltpu.VMEM((rows, chans), BF)
    weights = lambda n: (n, chans, chans)
    sems = pltpu.SemaphoreType.DMA((14,))

    ahead = ring(out_grad, 1)
    pair = swap(out_grad)
    again, pair = together((out_grad, pair))
    behind = ring(again, -1)
    sent, total, table, twists = call(
        prepare_kernel,
        (shape((PARTS, 2, CHANS, ROWS)), partial, shape(table.shape), shape(twists.shape, F32)),
        key_act, value_act, filter_taps, out_grad, out_weight, table, twists, pair,
        spaces="hhhhhhhv" + "hvvv",
        scratch=[
            held, held, pltpu.VMEM((rows, chans), F32), held, pltpu.VMEM(weights(2), BF),
            pltpu.VMEM((PARTS, 2, CHANS, ROWS), BF), sems,
        ],
        flops=270_000_000,
    )
    got = exchange(sent)
    ahead, total = together((ahead, total))
    far = ring(ahead, 1)
    ahead, behind = together((ahead, behind))
    total, later = call(
        first_mix_kernel, (partial, shape(weights(2))),
        out_weight, total, ahead, swap(ahead), behind, swap(behind),
        spaces="hvvvvv" + "vv",
        scratch=[pltpu.VMEM(weights(4), BF), sems], flops=7_000_000_000,
    )
    kept = call(
        early_kernel, shape((2 * KEPT, WIDE, ROWS), F32), got, table, twists,
        spaces="vvv" + "v",
        flops=1_200_000_000,
    )
    far, total, kept = together((far, total, kept))
    mix, sent = call(
        last_mix_kernel, (shape((rows, chans)), block),
        later, total, far, swap(far), gate_act,
        spaces="vvvvv" + "hv",
        scratch=[held, pltpu.SemaphoreType.DMA], flops=300_000_000_000,
    )
    got = exchange(sent)
    sent = call(
        late_kernel, shape((PARTS, 3, CHANS, ROWS)), got, kept, table, twists,
        spaces="vvvv" + "v", flops=1_200_000_000,
    )
    got = exchange(sent)
    return tuple(call(
        finish_kernel,
        (shape((rows, chans)), shape((rows, chans)), shape((rows, chans)), shape((rows, chans), F32)),
        got, mix, key_act, value_act,
        spaces="vvvv" + "hhhh",
        scratch=[held, held, held, pltpu.VMEM((rows, chans), F32), pltpu.SemaphoreType.DMA((4,))],
    ))


def solution(mesh):
    in_specs = (
        P("ctx", "tp"),
        P("ctx", "tp"),
        P("ctx", "tp"),
        P("ctx", "tp"),
        P("ctx", "tp"),
        P("tp", None),
    )
    out_specs = (P("ctx", "tp"), P("ctx", "tp"), P("ctx", "tp"), P("ctx", "tp"))
    return jax.shard_map(shards, mesh=mesh, in_specs=in_specs, out_specs=out_specs, check_vma=False)
```

```python
import math

import jax
import jax.numpy as jnp
import ml_dtypes
import numpy as np
from jax import lax
from jax.experimental import pallas as pl
from jax.experimental.pallas import tpu as pltpu
from jax.sharding import PartitionSpec as P

BF = jnp.bfloat16
F32 = jnp.float32
PARTS = 32
ROWS = 256
SIDE = PARTS // 2
CHANS = 16
TOKENS = PARTS * ROWS
HALF = CHANS // 2
WIDE = PARTS * HALF
SCALE = 1.0 / (math.sqrt(TOKENS) * TOKENS)


def tables():
    k1 = np.arange(PARTS)
    r = np.arange(ROWS)
    first = 2.0 * np.pi * (((4 * k1[:, None] + 1) * k1[None, :]) % (4 * PARTS)) / (4 * PARTS)
    twist = 2.0 * np.pi * (((4 * k1[:, None] + 1) * r[None, :]) % (4 * TOKENS)) / (4 * TOKENS)
    second = 2.0 * np.pi * ((r[:, None] * r[None, :]) % ROWS) / ROWS
    eye = np.eye(HALF)
    spread_re, spread_im = np.kron(np.cos(first), eye), np.kron(-np.sin(first), eye)
    gather = np.concatenate([spread_re.T, spread_im.T], 1)
    cos, sin = np.cos(second), np.sin(second)
    ahead = np.block([[cos, -sin], [sin, cos]])
    packed = np.concatenate([ahead, gather, np.concatenate([spread_re, spread_im], 1)], 0)
    twists = np.stack([np.cos(twist), np.sin(twist)])
    return packed.astype(ml_dtypes.bfloat16), twists.astype(np.float32)


def dot(a, b):
    return lax.dot_general(a, b, (((1,), (0,)), ((), ())), preferred_element_type=F32)


def dot_t(a, b):
    return lax.dot_general(a, b, (((1,), (1,)), ((), ())), preferred_element_type=F32)


def widen(twists):
    return [
        jnp.broadcast_to(twists[n][:, None, :], (PARTS, HALF, ROWS)).reshape(WIDE, ROWS)
        for n in range(2)
    ]


def first_stage(signals, spread, twists):
    cos, sin = twists[0], twists[1]
    turned = []
    for signal in signals:
        re = dot(spread[:, :WIDE], signal)
        im = dot(spread[:, WIDE:], signal)
        turned.append(
            jnp.concatenate([(re * cos + im * sin).astype(BF), (im * cos - re * sin).astype(BF)], 1)
        )
    return jnp.concatenate(turned, 0)


def inverses(pairs, ahead, gather, twists):
    rows = [jnp.concatenate([re.astype(BF), minus_im.astype(BF)], 1) for re, minus_im in pairs]
    out = dot(jnp.concatenate(rows, 0), ahead[...])
    cos, sin = twists[0], twists[1]
    results = []
    for n in range(len(pairs)):
        re = out[n * WIDE : (n + 1) * WIDE, :ROWS]
        minus_im = out[n * WIDE : (n + 1) * WIDE, ROWS:]
        turned_re = (re * cos + minus_im * sin).astype(BF)
        turned_im = (re * sin - minus_im * cos).astype(BF)
        back = dot(gather[...], jnp.concatenate([turned_re, turned_im], 0))
        results.append((back * SCALE).reshape(PARTS, HALF, ROWS))
    return results


def load_tables(table, twists, held, held_twists, sems):
    first = 2 * ROWS + WIDE
    ends = [
        (table.at[first:], held.at[first:]),
        (twists, held_twists),
        (table.at[: 2 * ROWS], held.at[: 2 * ROWS]),
        (table.at[2 * ROWS : first], held.at[2 * ROWS : first]),
    ]
    loads = [pltpu.make_async_copy(*pair, sems.at[n]) for n, pair in enumerate(ends)]
    for load in loads:
        load.start()
    parts = (held.at[first:], held.at[: 2 * ROWS], held.at[2 * ROWS : first])
    return loads, parts


def halves(block):
    rows = block.astype(F32).reshape(PARTS, 2, HALF, ROWS)
    return [rows[:, half].reshape(WIDE, ROWS).astype(BF) for half in range(2)]


def whole(parts):
    return jnp.stack(parts, 1).reshape(PARTS, CHANS, ROWS).astype(BF)


KEPT = 4
TABLE = 4
CONV, TABLES = 8, 10


def pick_kernel(got, stay, away, sems):
    copies = [pltpu.make_async_copy(got.at[:, n], out, sems.at[n]) for n, out in enumerate((stay, away))]
    for copy in copies:
        copy.start()
    for copy in copies:
        copy.wait()


def start_all(ends, sems):
    copies = [pltpu.make_async_copy(*pair, sems.at[n]) for n, pair in enumerate(ends)]
    for copy in copies:
        copy.start()
    return copies


def wait_all(copies):
    for copy in copies:
        copy.wait()


SPREAD = slice(2 * ROWS + WIDE, 2 * ROWS + 2 * WIDE)
AHEAD = slice(0, 2 * ROWS)
GATHER = slice(2 * ROWS, 2 * ROWS + WIDE)


class Parts:
    def __init__(self, refs):
        self.where = [(ref, n) for ref in refs for n in range(ref.shape[0])]

    def put(self, index, value):
        ref, n = self.where[index]
        ref[n] = value.astype(ref.dtype)

    def get(self, index, dtype=F32):
        ref, n = self.where[index]
        return ref[n].astype(dtype)


def early_kernel(near, other, table, twists, *refs):
    kept, (kept_twists, both, tab, tw, sems) = Parts(refs[:-5]), refs[-5:]
    side = lax.div(lax.axis_index("ctx"), SIDE)
    ends = [(near, both.at[side]), (other, both.at[1 - side]), (table, tab), (twists, tw)]
    wait_all(start_all(ends, sems))
    got = both[...].reshape(PARTS, 2, CHANS, ROWS)
    signals = halves(got[:, 0]) + halves(got[:, 1])
    wide = widen(tw)
    out = dot(first_stage(signals, tab.at[SPREAD], wide), tab[AHEAD, :])
    pairs = []
    for half in range(2):
        x, h = out[half * WIDE : (half + 1) * WIDE], out[(half + 2) * WIDE : (half + 3) * WIDE]
        xr, xi, hr, hi = x[:, :ROWS], x[:, ROWS:], h[:, :ROWS], h[:, ROWS:]
        for n, part in enumerate((xr, xi, hr, hi)):
            kept.put(half * KEPT + n, part)
        pairs.append((hr * xr - hi * xi, -(hr * xi + hi * xr)))
    for half, conv in enumerate(inverses(pairs, tab.at[AHEAD], tab.at[GATHER], wide)):
        kept.put(CONV + half, conv.reshape(WIDE, ROWS))
    for side in range(2):
        for n in range(TABLE):
            rows, cols = slice(n * ROWS, (n + 1) * ROWS), slice(side * ROWS, (side + 1) * ROWS)
            kept.put(TABLES + side * TABLE + n, tab[rows, cols])
    kept_twists[...] = tw[...]


def late_kernel(got, *refs):
    kept, (twists, out) = Parts(refs[:-2]), refs[-2:]

    def table(start, stop):
        sides = [
            jnp.concatenate([kept.get(TABLES + side * TABLE + n, BF) for n in range(start, stop)], 0)
            for side in range(2)
        ]
        return jnp.concatenate(sides, 1)

    ahead, gather, spread = table(0, 2), table(2, 3), table(3, 4)
    twists = widen(twists)
    out[:, 0] = whole([kept.get(CONV + n).reshape(PARTS, HALF, ROWS) for n in range(2)])
    grad = dot(first_stage(halves(got[...]), spread, twists), ahead)
    pairs = []
    for half in range(2):
        g = grad[half * WIDE : (half + 1) * WIDE]
        gr, gi = g[:, :ROWS], g[:, ROWS:]
        xr, xi, hr, hi = (kept.get(half * KEPT + n) for n in range(KEPT))
        pairs.append((hr * gr + hi * gi, hi * gr - hr * gi))
        pairs.append((xr * gr + xi * gi, xi * gr - xr * gi))
    results = inverses(pairs, ahead, gather, twists)
    out[:, 1] = whole([results[0], results[2]])
    out[:, 2] = whole([results[1], results[3]])


def columns(step, flip, width):
    holder = lax.axis_index("tp") ^ flip
    count = lax.axis_size("tp")
    way = 1 - 2 * lax.rem(holder, 2)
    owner = lax.rem(holder - 2 * step * way + count, count)
    return pl.ds(pl.multiple_of(owner * width, width), width)


def prepare_kernel(
    key, value, taps, own, weight, pair, out, total, k, v, t, o, w, sent, sems
):
    width = own.shape[1]
    loads = [(key, k), (value, v), (taps, t), (own, o)]
    loads += [(weight.at[:, columns(0, flip, width)], w.at[flip]) for flip in range(2)]
    loads = [pltpu.make_async_copy(*ends, sems.at[n]) for n, ends in enumerate(loads)]
    for load in loads:
        load.start()
    for load in loads[:2]:
        load.wait()
    inner = k[...].astype(F32) * v[...].astype(F32)
    side = lax.div(lax.axis_index("ctx"), SIDE)

    def place(signal, block):
        parts = block.T.astype(BF).reshape(2, SIDE, CHANS, ROWS)
        for owner in range(2):
            sent[:, owner ^ side, signal] = parts[owner]

    place(0, inner)
    loads[2].wait()
    place(1, t[...])
    store = pltpu.make_async_copy(sent, out, sems.at[6])
    store.start()
    for load in loads[3:]:
        load.wait()
    total[...] = dot_t(o[...], w[0]) + dot_t(pair[...], w[1])
    store.wait()


def first_mix_kernel(weight, before, ahead, ahead_pair, behind, behind_pair, total, later, w, sems):
    width = ahead.shape[1]
    loads = []
    for n, (step, flip) in enumerate(((1, 0), (1, 1), (-1, 0), (-1, 1), (2, 0), (2, 1))):
        target = w.at[n] if n < 4 else later.at[n - 4]
        loads.append(
            pltpu.make_async_copy(weight.at[:, columns(step, flip, width)], target, sems.at[n])
        )
        loads[n].start()
    sums = before[...]
    for n, block in enumerate((ahead, ahead_pair, behind, behind_pair)):
        loads[n].wait()
        sums = sums + dot_t(block[...], w[n])
    total[...] = sums
    loads[4].wait()
    loads[5].wait()


def last_mix_kernel(weight, total, far, far_pair, gate, mix, out, mixed, grads, sems):
    width = total.shape[1] // 2
    copies = []
    for n in range(2):
        chans = slice(n * width, (n + 1) * width)
        sums = total[:, chans] + dot_t(far[...], weight[0, chans, :])
        sums = sums + dot_t(far_pair[...], weight[1, chans, :])
        mixed[n] = sums.astype(BF)
        grad = mixed[n].astype(F32) * gate[:, chans].astype(F32)
        grads[n] = grad.T.astype(BF).reshape(PARTS // 2, CHANS, ROWS)
        copies.append(
            pltpu.make_async_copy(grads.at[n], out.at[n * PARTS // 2 : (n + 1) * PARTS // 2], sems.at[n])
        )
        copies[-1].start()
        copies.append(pltpu.make_async_copy(mixed.at[n], mix.at[:, chans], sems.at[2 + n]))
        copies[-1].start()
    for copy in copies:
        copy.wait()


def finish_kernel(got, mix, key, value, *refs):
    outs, results, sems = refs[:4], refs[4:8], refs[8]

    def result(slot):
        return got[:, slot].reshape(PARTS * CHANS, ROWS).astype(F32).T

    def store(n):
        copy = pltpu.make_async_copy(results[n], outs[n], sems.at[n])
        copy.start()
        return copy

    results[3][...] = result(2)
    copies = [store(3)]
    inner = result(1)
    results[1][...] = (inner * value[...].astype(F32)).astype(BF)
    copies.append(store(1))
    results[2][...] = (inner * key[...].astype(F32)).astype(BF)
    copies.append(store(2))
    results[0][...] = (mix[...].astype(F32) * result(0)).astype(BF)
    copies.append(store(0))
    for copy in copies:
        copy.wait()


PARAMS = pltpu.CompilerParams(vmem_limit_bytes=40 * 1024 * 1024)


def call(kernel, outs, *args, spaces, scratch=(), flops=0):
    leaves = jax.tree.leaves(outs)
    nbytes = sum(a.size * a.dtype.itemsize for a in (*args, *leaves))
    spaces = [pltpu.HBM if letter == "h" else pltpu.VMEM for letter in spaces]
    specs = [pl.BlockSpec(memory_space=space) for space in spaces]
    args = [pltpu.with_memory_space_constraint(a, space) for a, space in zip(args, spaces)]
    placed = [space(a.shape, a.dtype) for a, space in zip(leaves, spaces[len(args) :])]
    results = pl.pallas_call(
        kernel,
        out_shape=placed,
        in_specs=specs[: len(args)],
        out_specs=specs[len(args) :],
        scratch_shapes=scratch,
        compiler_params=PARAMS,
        cost_estimate=pl.CostEstimate(flops=flops, bytes_accessed=nbytes, transcendentals=0),
    )(*args)
    return results if isinstance(outs, tuple) else results[0]


def shape(dims, dtype=BF):
    return jax.ShapeDtypeStruct(dims, dtype)


def shards(out_grad, gate_act, key_act, value_act, filter_taps, out_weight):
    count = lax.axis_size("tp")
    rows, chans = gate_act.shape

    def ring(block, way):
        hops = [(i, (i + way * (2 - 4 * (i % 2))) % count) for i in range(count)]
        return lax.ppermute(block, "tp", hops)

    def swap(block):
        return lax.ppermute(block, "tp", [(i, i ^ 1) for i in range(count)])

    def exchange(block):
        return lax.all_to_all(block, "ctx", split_axis=0, concat_axis=0, tiled=True)

    table, twists = (jnp.asarray(t) for t in tables())
    together = lax.optimization_barrier
    block = shape((PARTS, CHANS, ROWS))
    partial = shape((rows, chans), F32)
    held = pltpu.VMEM((rows, chans), BF)
    weights = lambda n: (n, chans, chans)
    sems = pltpu.SemaphoreType.DMA((7,))

    tables_held = [pltpu.VMEM(table.shape, BF), pltpu.VMEM(twists.shape, F32)]

    ahead = ring(out_grad, 1)
    pair = swap(out_grad)
    again, pair = together((out_grad, pair))
    behind = ring(again, -1)
    sent, total = call(
        prepare_kernel,
        (shape((SIDE, 2, 2, CHANS, ROWS)), partial),
        key_act, value_act, filter_taps, out_grad, out_weight, pair,
        spaces="hhhhhv" + "hv",
        scratch=[
            held, held, pltpu.VMEM((rows, chans), F32), held, pltpu.VMEM(weights(2), BF),
            pltpu.VMEM((SIDE, 2, 2, CHANS, ROWS), BF), sems,
        ],
        flops=270_000_000,
    )
    planes = [list(range(SIDE)), list(range(SIDE, PARTS))]
    near = lax.all_to_all(
        sent, "ctx", split_axis=0, concat_axis=0, tiled=True, axis_index_groups=planes
    )
    ahead, total = together((ahead, total))
    far = ring(ahead, 1)
    ahead, behind = together((ahead, behind))
    total, later = call(
        first_mix_kernel, (partial, shape(weights(2))),
        out_weight, total, ahead, swap(ahead), behind, swap(behind),
        spaces="hvvvvv" + "vv",
        scratch=[pltpu.VMEM(weights(4), BF), sems], flops=7_000_000_000,
    )
    near, away = call(
        pick_kernel, (shape((SIDE, 2, CHANS, ROWS)), shape((SIDE, 2, CHANS, ROWS))), near,
        spaces="v" + "hh", scratch=[sems],
    )
    far, total, away = together((far, total, away))
    other = lax.ppermute(away, "ctx", [(i, (i + SIDE) % PARTS) for i in range(PARTS)])
    mix, sent = call(
        last_mix_kernel, (shape((rows, chans)), block),
        later, total, far, swap(far), gate_act,
        spaces="vvvvv" + "hh",
        scratch=[
            pltpu.VMEM((2, rows, chans // 2), BF), pltpu.VMEM((2, PARTS // 2, CHANS, ROWS), BF), sems,
        ],
        flops=300_000_000_000,
    )
    got = exchange(sent)
    kept = call(
        early_kernel, (shape((10, WIDE, ROWS)), shape((8, WIDE, ROWS)), shape(twists.shape, F32)), near, other, table, twists,
        spaces="hhhh" + "vvv",
        scratch=[pltpu.VMEM((2, SIDE, 2, CHANS, ROWS), BF), *tables_held, sems],
        flops=20_000_000_000,
    )
    sent = call(
        late_kernel, shape((PARTS, 3, CHANS, ROWS)), got, *kept,
        spaces="v" + "vvv" + "v", flops=1_200_000_000,
    )
    got = exchange(sent)
    return tuple(call(
        finish_kernel,
        (shape((rows, chans)), shape((rows, chans)), shape((rows, chans)), shape((rows, chans), F32)),
        got, mix, key_act, value_act,
        spaces="vvvv" + "hhhh",
        scratch=[held, held, held, pltpu.VMEM((rows, chans), F32), pltpu.SemaphoreType.DMA((4,))],
    ))


def solution(mesh):
    in_specs = (
        P("ctx", "tp"),
        P("ctx", "tp"),
        P("ctx", "tp"),
        P("ctx", "tp"),
        P("ctx", "tp"),
        P("tp", None),
    )
    out_specs = (P("ctx", "tp"), P("ctx", "tp"), P("ctx", "tp"), P("ctx", "tp"))
    return jax.shard_map(shards, mesh=mesh, in_specs=in_specs, out_specs=out_specs, check_vma=False)
```

```python
import math

import jax
import jax.numpy as jnp
import ml_dtypes
import numpy as np
from jax import lax
from jax.experimental import pallas as pl
from jax.experimental.pallas import tpu as pltpu
from jax.sharding import PartitionSpec as P

BF = jnp.bfloat16
F32 = jnp.float32
PARTS = 32
ROWS = 256
SIDE = PARTS // 2
CHANS = 16
TOKENS = PARTS * ROWS
HALF = CHANS // 2
WIDE = PARTS * HALF
SCALE = 1.0 / (math.sqrt(TOKENS) * TOKENS)


def tables():
    k1 = np.arange(PARTS)
    r = np.arange(ROWS)
    first = 2.0 * np.pi * (((4 * k1[:, None] + 1) * k1[None, :]) % (4 * PARTS)) / (4 * PARTS)
    twist = 2.0 * np.pi * (((4 * k1[:, None] + 1) * r[None, :]) % (4 * TOKENS)) / (4 * TOKENS)
    second = 2.0 * np.pi * ((r[:, None] * r[None, :]) % ROWS) / ROWS
    eye = np.eye(HALF)
    spread_re, spread_im = np.kron(np.cos(first), eye), np.kron(-np.sin(first), eye)
    gather = np.concatenate([spread_re.T, spread_im.T], 1)
    cos, sin = np.cos(second), np.sin(second)
    ahead = np.block([[cos, -sin], [sin, cos]])
    packed = np.concatenate([ahead, gather, np.concatenate([spread_re, spread_im], 1)], 0)
    twists = np.stack([np.cos(twist), np.sin(twist)])
    return packed.astype(ml_dtypes.bfloat16), twists.astype(np.float32)


def dot(a, b):
    return lax.dot_general(a, b, (((1,), (0,)), ((), ())), preferred_element_type=F32)


def dot_t(a, b):
    return lax.dot_general(a, b, (((1,), (1,)), ((), ())), preferred_element_type=F32)


def widen(twists):
    return [
        jnp.broadcast_to(twists[n][:, None, :], (PARTS, HALF, ROWS)).reshape(WIDE, ROWS)
        for n in range(2)
    ]


def first_stage(signals, spread, twists):
    cos, sin = twists[0], twists[1]
    turned = []
    for signal in signals:
        re = dot(spread[:, :WIDE], signal)
        im = dot(spread[:, WIDE:], signal)
        turned.append(
            jnp.concatenate([(re * cos + im * sin).astype(BF), (im * cos - re * sin).astype(BF)], 1)
        )
    return jnp.concatenate(turned, 0)


def inverses(pairs, ahead, gather, twists):
    rows = [jnp.concatenate([re.astype(BF), minus_im.astype(BF)], 1) for re, minus_im in pairs]
    out = dot(jnp.concatenate(rows, 0), ahead[...])
    cos, sin = twists[0], twists[1]
    results = []
    for n in range(len(pairs)):
        re = out[n * WIDE : (n + 1) * WIDE, :ROWS]
        minus_im = out[n * WIDE : (n + 1) * WIDE, ROWS:]
        turned_re = (re * cos + minus_im * sin).astype(BF)
        turned_im = (re * sin - minus_im * cos).astype(BF)
        back = dot(gather[...], jnp.concatenate([turned_re, turned_im], 0))
        results.append((back * SCALE).reshape(PARTS, HALF, ROWS))
    return results


def load_tables(table, twists, held, held_twists, sems):
    first = 2 * ROWS + WIDE
    ends = [
        (table.at[first:], held.at[first:]),
        (twists, held_twists),
        (table.at[: 2 * ROWS], held.at[: 2 * ROWS]),
        (table.at[2 * ROWS : first], held.at[2 * ROWS : first]),
    ]
    loads = [pltpu.make_async_copy(*pair, sems.at[n]) for n, pair in enumerate(ends)]
    for load in loads:
        load.start()
    parts = (held.at[first:], held.at[: 2 * ROWS], held.at[2 * ROWS : first])
    return loads, parts


def halves(block):
    rows = block.astype(F32).reshape(PARTS, 2, HALF, ROWS)
    return [rows[:, half].reshape(WIDE, ROWS).astype(BF) for half in range(2)]


def whole(parts):
    return jnp.stack(parts, 1).reshape(PARTS, CHANS, ROWS).astype(BF)


KEPT = 4
TABLE = 4
CONV, TABLES = 8, 10


def pick_kernel(got, stay, away, sems):
    copies = [pltpu.make_async_copy(got.at[:, n], out, sems.at[n]) for n, out in enumerate((stay, away))]
    for copy in copies:
        copy.start()
    for copy in copies:
        copy.wait()


def start_all(ends, sems):
    copies = [pltpu.make_async_copy(*pair, sems.at[n]) for n, pair in enumerate(ends)]
    for copy in copies:
        copy.start()
    return copies


def wait_all(copies):
    for copy in copies:
        copy.wait()


SPREAD = slice(2 * ROWS + WIDE, 2 * ROWS + 2 * WIDE)
AHEAD = slice(0, 2 * ROWS)
GATHER = slice(2 * ROWS, 2 * ROWS + WIDE)


class Parts:
    def __init__(self, refs):
        self.where = [(ref, n) for ref in refs for n in range(ref.shape[0])]

    def put(self, index, value):
        ref, n = self.where[index]
        ref[n] = value.astype(ref.dtype)

    def get(self, index, dtype=F32):
        ref, n = self.where[index]
        return ref[n].astype(dtype)


def early_kernel(near, other, table, twists, *refs):
    kept, (kept_twists, both, tab, tw, sems) = Parts(refs[:-5]), refs[-5:]
    side = lax.div(lax.axis_index("ctx"), SIDE)
    ends = [(near, both.at[side]), (other, both.at[1 - side]), (table, tab), (twists, tw)]
    wait_all(start_all(ends, sems))
    got = both[...].reshape(PARTS, 2, CHANS, ROWS)
    signals = halves(got[:, 0]) + halves(got[:, 1])
    wide = widen(tw)
    out = dot(first_stage(signals, tab.at[SPREAD], wide), tab[AHEAD, :])
    pairs = []
    for half in range(2):
        x, h = out[half * WIDE : (half + 1) * WIDE], out[(half + 2) * WIDE : (half + 3) * WIDE]
        xr, xi, hr, hi = x[:, :ROWS], x[:, ROWS:], h[:, :ROWS], h[:, ROWS:]
        for n, part in enumerate((xr, xi, hr, hi)):
            kept.put(half * KEPT + n, part)
        pairs.append((hr * xr - hi * xi, -(hr * xi + hi * xr)))
    for half, conv in enumerate(inverses(pairs, tab.at[AHEAD], tab.at[GATHER], wide)):
        kept.put(CONV + half, conv.reshape(WIDE, ROWS))
    for side in range(2):
        for n in range(TABLE):
            rows, cols = slice(n * ROWS, (n + 1) * ROWS), slice(side * ROWS, (side + 1) * ROWS)
            kept.put(TABLES + side * TABLE + n, tab[rows, cols])
    kept_twists[...] = tw[...]


def late_kernel(got, *refs):
    kept, (twists, out) = Parts(refs[:-2]), refs[-2:]

    def table(start, stop):
        sides = [
            jnp.concatenate([kept.get(TABLES + side * TABLE + n, BF) for n in range(start, stop)], 0)
            for side in range(2)
        ]
        return jnp.concatenate(sides, 1)

    ahead, gather, spread = table(0, 2), table(2, 3), table(3, 4)
    twists = widen(twists)
    out[:, 0] = whole([kept.get(CONV + n).reshape(PARTS, HALF, ROWS) for n in range(2)])
    grad = dot(first_stage(halves(got[...]), spread, twists), ahead)
    pairs = []
    for half in range(2):
        g = grad[half * WIDE : (half + 1) * WIDE]
        gr, gi = g[:, :ROWS], g[:, ROWS:]
        xr, xi, hr, hi = (kept.get(half * KEPT + n) for n in range(KEPT))
        pairs.append((hr * gr + hi * gi, hi * gr - hr * gi))
        pairs.append((xr * gr + xi * gi, xi * gr - xr * gi))
    results = inverses(pairs, ahead, gather, twists)
    out[:, 1] = whole([results[0], results[2]])
    out[:, 2] = whole([results[1], results[3]])


def columns(step, flip, width):
    holder = lax.axis_index("tp") ^ flip
    count = lax.axis_size("tp")
    way = 1 - 2 * lax.rem(holder, 2)
    owner = lax.rem(holder - 2 * step * way + count, count)
    return pl.ds(pl.multiple_of(owner * width, width), width)


def prepare_kernel(
    key, value, taps, own, weight, pair, out, total, k, v, t, o, w, sent, sems
):
    width = own.shape[1]
    loads = [(key, k), (value, v), (taps, t), (own, o)]
    loads += [(weight.at[:, columns(0, flip, width)], w.at[flip]) for flip in range(2)]
    loads = [pltpu.make_async_copy(*ends, sems.at[n]) for n, ends in enumerate(loads)]
    for load in loads:
        load.start()
    for load in loads[:2]:
        load.wait()
    inner = k[...].astype(F32) * v[...].astype(F32)
    side = lax.div(lax.axis_index("ctx"), SIDE)

    def place(signal, block):
        parts = block.T.astype(BF).reshape(2, SIDE, CHANS, ROWS)
        for owner in range(2):
            sent[:, owner ^ side, signal] = parts[owner]

    place(0, inner)
    loads[2].wait()
    place(1, t[...])
    store = pltpu.make_async_copy(sent, out, sems.at[6])
    store.start()
    for load in loads[3:]:
        load.wait()
    total[...] = dot_t(o[...], w[0]) + dot_t(pair[...], w[1])
    store.wait()


def first_mix_kernel(weight, before, ahead, ahead_pair, behind, behind_pair, total, later, w, sems):
    width = ahead.shape[1]
    loads = []
    for n, (step, flip) in enumerate(((1, 0), (1, 1), (-1, 0), (-1, 1), (2, 0), (2, 1))):
        target = w.at[n] if n < 4 else later.at[n - 4]
        loads.append(
            pltpu.make_async_copy(weight.at[:, columns(step, flip, width)], target, sems.at[n])
        )
        loads[n].start()
    sums = before[...]
    for n, block in enumerate((ahead, ahead_pair, behind, behind_pair)):
        loads[n].wait()
        sums = sums + dot_t(block[...], w[n])
    total[...] = sums
    loads[4].wait()
    loads[5].wait()


def last_mix_kernel(weight, total, far, far_pair, gate, mix, out, mixed, grads, sems):
    width = total.shape[1] // 2
    copies = []
    for n in range(2):
        chans = slice(n * width, (n + 1) * width)
        sums = total[:, chans] + dot_t(far[...], weight[0, chans, :])
        sums = sums + dot_t(far_pair[...], weight[1, chans, :])
        mixed[n] = sums.astype(BF)
        grad = mixed[n].astype(F32) * gate[:, chans].astype(F32)
        grads[n] = grad.T.astype(BF).reshape(PARTS // 2, CHANS, ROWS)
        copies.append(
            pltpu.make_async_copy(grads.at[n], out.at[n * PARTS // 2 : (n + 1) * PARTS // 2], sems.at[n])
        )
        copies[-1].start()
        copies.append(pltpu.make_async_copy(mixed.at[n], mix.at[:, chans], sems.at[2 + n]))
        copies[-1].start()
    for copy in copies:
        copy.wait()


def finish_kernel(got, mix, key, value, *refs):
    outs, results, sems = refs[:4], refs[4:8], refs[8]

    def result(slot):
        return got[:, slot].reshape(PARTS * CHANS, ROWS).astype(F32).T

    def store(n):
        copy = pltpu.make_async_copy(results[n], outs[n], sems.at[n])
        copy.start()
        return copy

    results[3][...] = result(2)
    copies = [store(3)]
    inner = result(1)
    results[1][...] = (inner * value[...].astype(F32)).astype(BF)
    copies.append(store(1))
    results[2][...] = (inner * key[...].astype(F32)).astype(BF)
    copies.append(store(2))
    results[0][...] = (mix[...].astype(F32) * result(0)).astype(BF)
    copies.append(store(0))
    for copy in copies:
        copy.wait()


PARAMS = pltpu.CompilerParams(vmem_limit_bytes=40 * 1024 * 1024)


def call(kernel, outs, *args, spaces, scratch=(), flops=0):
    leaves = jax.tree.leaves(outs)
    nbytes = sum(a.size * a.dtype.itemsize for a in (*args, *leaves))
    spaces = [pltpu.HBM if letter == "h" else pltpu.VMEM for letter in spaces]
    specs = [pl.BlockSpec(memory_space=space) for space in spaces]
    args = [pltpu.with_memory_space_constraint(a, space) for a, space in zip(args, spaces)]
    placed = [space(a.shape, a.dtype) for a, space in zip(leaves, spaces[len(args) :])]
    results = pl.pallas_call(
        kernel,
        out_shape=placed,
        in_specs=specs[: len(args)],
        out_specs=specs[len(args) :],
        scratch_shapes=scratch,
        compiler_params=PARAMS,
        cost_estimate=pl.CostEstimate(flops=flops, bytes_accessed=nbytes, transcendentals=0),
    )(*args)
    return results if isinstance(outs, tuple) else results[0]


def shape(dims, dtype=BF):
    return jax.ShapeDtypeStruct(dims, dtype)


def shards(out_grad, gate_act, key_act, value_act, filter_taps, out_weight):
    count = lax.axis_size("tp")
    rows, chans = gate_act.shape

    def ring(block, way):
        hops = [(i, (i + way * (2 - 4 * (i % 2))) % count) for i in range(count)]
        return lax.ppermute(block, "tp", hops)

    def swap(block):
        return lax.ppermute(block, "tp", [(i, i ^ 1) for i in range(count)])

    def exchange(block):
        return lax.all_to_all(block, "ctx", split_axis=0, concat_axis=0, tiled=True)

    table, twists = (jnp.asarray(t) for t in tables())
    together = lax.optimization_barrier
    block = shape((PARTS, CHANS, ROWS))
    partial = shape((rows, chans), F32)
    held = pltpu.VMEM((rows, chans), BF)
    weights = lambda n: (n, chans, chans)
    sems = pltpu.SemaphoreType.DMA((7,))

    tables_held = [pltpu.VMEM(table.shape, BF), pltpu.VMEM(twists.shape, F32)]

    ahead = ring(out_grad, 1)
    pair = swap(out_grad)

    behind = ring(out_grad, -1)
    sent, total = call(
        prepare_kernel,
        (shape((SIDE, 2, 2, CHANS, ROWS)), partial),
        key_act, value_act, filter_taps, out_grad, out_weight, pair,
        spaces="hhhhhv" + "hv",
        scratch=[
            held, held, pltpu.VMEM((rows, chans), F32), held, pltpu.VMEM(weights(2), BF),
            pltpu.VMEM((SIDE, 2, 2, CHANS, ROWS), BF), sems,
        ],
        flops=270_000_000,
    )
    planes = [list(range(SIDE)), list(range(SIDE, PARTS))]
    near = lax.all_to_all(
        sent, "ctx", split_axis=0, concat_axis=0, tiled=True, axis_index_groups=planes
    )
    ahead, total = together((ahead, total))
    far = ring(ahead, 1)
    ahead, behind = together((ahead, behind))
    near, away = call(
        pick_kernel, (shape((SIDE, 2, CHANS, ROWS)), shape((SIDE, 2, CHANS, ROWS))), near,
        spaces="v" + "hh", scratch=[sems],
    )
    total, away = together((total, away))
    total, later = call(
        first_mix_kernel, (partial, shape(weights(2))),
        out_weight, total, ahead, swap(ahead), behind, swap(behind),
        spaces="hvvvvv" + "vv",
        scratch=[pltpu.VMEM(weights(4), BF), sems], flops=1,
    )
    far, total, away = together((far, total, away))
    other = lax.ppermute(away, "ctx", [(i, (i + SIDE) % PARTS) for i in range(PARTS)])
    mix, sent = call(
        last_mix_kernel, (shape((rows, chans)), block),
        later, total, far, swap(far), gate_act,
        spaces="vvvvv" + "hh",
        scratch=[
            pltpu.VMEM((2, rows, chans // 2), BF), pltpu.VMEM((2, PARTS // 2, CHANS, ROWS), BF), sems,
        ],
        flops=300_000_000_000,
    )
    got = exchange(sent)
    kept = call(
        early_kernel, (shape((10, WIDE, ROWS)), shape((8, WIDE, ROWS)), shape(twists.shape, F32)), near, other, table, twists,
        spaces="hhhh" + "vvv",
        scratch=[pltpu.VMEM((2, SIDE, 2, CHANS, ROWS), BF), *tables_held, sems],
        flops=20_000_000_000,
    )
    sent = call(
        late_kernel, shape((PARTS, 3, CHANS, ROWS)), got, *kept,
        spaces="v" + "vvv" + "v", flops=1_200_000_000,
    )
    got = exchange(sent)
    return tuple(call(
        finish_kernel,
        (shape((rows, chans)), shape((rows, chans)), shape((rows, chans)), shape((rows, chans), F32)),
        got, mix, key_act, value_act,
        spaces="vvvv" + "hhhh",
        scratch=[held, held, held, pltpu.VMEM((rows, chans), F32), pltpu.SemaphoreType.DMA((4,))],
    ))


def solution(mesh):
    in_specs = (
        P("ctx", "tp"),
        P("ctx", "tp"),
        P("ctx", "tp"),
        P("ctx", "tp"),
        P("ctx", "tp"),
        P("tp", None),
    )
    out_specs = (P("ctx", "tp"), P("ctx", "tp"), P("ctx", "tp"), P("ctx", "tp"))
    return jax.shard_map(shards, mesh=mesh, in_specs=in_specs, out_specs=out_specs, check_vma=False)
```
